512 devices in a mesh: gz: 32 (over x, z), gx: 8 (over y), gy: 2 (over core).
Axes of the slice: x: 4, y: 8, z: 8, core: 2. Of those that a mesh axis runs over, the one named last changes fastest.
Arguments:
- solution_in: float32 [768, 64, 256], P('gz', 'gx', 'gy'), may hold values from -6 to 6
- residual_in: float32 [768, 64, 256], P('gz', 'gx', 'gy'), may hold values from -13 to 13
- direction_in: float32 [768, 64, 256], P('gz', 'gx', 'gy'), may hold values from -17 to 17
- cond_x: float32 [768, 64, 256], P('gz', 'gx', 'gy'), may hold values from 0.05 to 0.5
- cond_y: float32 [768, 64, 256], P('gz', 'gx', 'gy'), may hold values from 0.05 to 0.5
- cond_z: float32 [768, 64, 256], P('gz', 'gx', 'gy'), may hold values from 1500 to 6000
- helmholtz: float32 [768, 64, 256], P('gz', 'gx', 'gy'), may hold values from 0.1 to 0.6
Outputs:
- solution_out: float32 [768, 64, 256], P('gz', 'gx', 'gy')
- residual_out: float32 [768, 64, 256], P('gz', 'gx', 'gy')
- direction_out: float32 [768, 64, 256], P('gz', 'gx', 'gy')
The draws below stay inside these ranges and needn't reach their ends.
All inputs are finite; a program needn't handle non-finite values.
Results may differ from the reference program's by a relative error of at most 0.00035.
Values sent between devices are 32-bit elements; how exact they have to be, the bound alone decides.
No kernel may reach another device: no remote copies, remote signals or barrier semaphores. Data moves between devices by JAX's collectives and lax.ppermute only.
A program may use at most 64 MiB of HBM per device.

```python
import math
import jax
import jax.numpy as jnp
from jax import lax

NZ = 768
NX = 64
NY = 256


def shared_values(key):
    return jnp.clip(jax.random.normal(key, (NZ, NX, NY), jnp.float32), -4.0, 4.0)


def vertical_profile():
    height = jnp.arange(NZ, dtype=jnp.float32) / (NZ - 1)
    return (1.0 + 2.0 * height)[:, None, None]


def draw_residual_in(key, part):
    common = shared_values(key)
    column = common[:1]
    result = (0.6 * common + 0.45 * column) * vertical_profile()
    return result.astype(jnp.float32)


def draw_direction_in(key, part):
    common = shared_values(key)
    column = common[:1]
    key = jax.random.fold_in(key, 23)
    first_key, second_key = jax.random.split(key)
    extra = jnp.clip(jax.random.normal(first_key, (1, NX, NY), jnp.float32), -4.0, 4.0)
    rough = jnp.clip(jax.random.normal(second_key, (NZ, NX, NY), jnp.float32), -4.0, 4.0)
    result = (0.8 * column + 0.6 * extra) * vertical_profile() + 0.02 * rough
    return result.astype(jnp.float32)


def levels(own_key, shape, cuts, smallest, high):
    def one(dim, parts):
        draws = jax.random.uniform(jax.random.fold_in(jax.random.fold_in(own_key, 6), dim), (parts,), jnp.float32, smallest / len(cuts), high / len(cuts))
        return jnp.repeat(jnp.exp(draws), shape[dim] // parts).reshape((-1,) + (1,) * (len(shape) - dim - 1))

    factor_of = one(*cuts[0])
    for cut in cuts[1:]:
        factor_of = factor_of * one(*cut)
    return factor_of


def normal_values(own_key, shape, deviation, reach, cuts=(), kind=jnp.bfloat16):
    values = deviation * jax.random.normal(own_key, shape, jnp.float32)
    if cuts:
        values = values * levels(own_key, shape, cuts, -0.22, 0.18)
    return jnp.clip(values, -reach, reach).astype(kind)


def setup_inputs(seed: int = 0) -> dict:
    seeds = jax.random.split(jax.random.key(seed), 8)
    solution_in = normal_values(seeds[0], (NZ, NX, NY), 1.0, 6.0, ((0, 32), (1, 8), (2, 2)), jnp.float32)
    residual_in = draw_residual_in(jax.random.fold_in(seeds[7], 71), 0)
    direction_in = draw_direction_in(jax.random.fold_in(seeds[7], 71), 0)
    cond_x = jnp.clip(jnp.exp(math.log(0.5) - 2.3025851 * jax.random.uniform(seeds[3], (NZ, NX, NY), jnp.float32) ** levels(seeds[3], (NZ, NX, NY), ((0, 32), (1, 8), (2, 2)), -0.2, 0.2)), 0.05, 0.5)
    cond_y = jnp.clip(jnp.exp(math.log(0.5) - 2.3025851 * jax.random.uniform(seeds[4], (NZ, NX, NY), jnp.float32) ** levels(seeds[4], (NZ, NX, NY), ((0, 32), (1, 8), (2, 2)), -0.2, 0.2)), 0.05, 0.5)
    cond_z = jnp.clip(jnp.exp(math.log(6000.0) - 1.3862944 * jax.random.uniform(seeds[5], (NZ, NX, NY), jnp.float32) ** levels(seeds[5], (NZ, NX, NY), ((0, 32), (1, 8), (2, 2)), -0.2, 0.2)), 1500.0, 6000.0)
    helmholtz = jnp.clip(jnp.exp(math.log(0.6) - 1.7917595 * jax.random.uniform(seeds[6], (NZ, NX, NY), jnp.float32) ** levels(seeds[6], (NZ, NX, NY), ((0, 32), (1, 8), (2, 2)), -0.2, 0.2)), 0.1, 0.6)
    return {"solution_in": solution_in, "residual_in": residual_in, "direction_in": direction_in, "cond_x": cond_x, "cond_y": cond_y, "cond_z": cond_z, "helmholtz": helmholtz}


def lower_of(values, axis_dim):
    extent = values.shape[axis_dim]
    padding = [(0, 0), (0, 0), (0, 0)]
    padding[axis_dim] = (1, 0)
    return lax.slice_in_dim(jnp.pad(values, padding), 0, extent, axis=axis_dim)


def upper_of(values, axis_dim):
    extent = values.shape[axis_dim]
    padding = [(0, 0), (0, 0), (0, 0)]
    padding[axis_dim] = (0, 1)
    return lax.slice_in_dim(jnp.pad(values, padding), 1, extent + 1, axis=axis_dim)


def operate(values, coeffs):
    cond_x, cond_y, cond_z, low_x, low_y, low_z, diagonal = coeffs
    result = diagonal * values - cond_x * upper_of(values, 1) - low_x * lower_of(values, 1)
    result = result - cond_y * upper_of(values, 2) - low_y * lower_of(values, 2)
    return result - cond_z * upper_of(values, 0) - low_z * lower_of(values, 0)


def tridiagonal(lower_coef, main_coef, upper_coef, source):
    def forward(running, row_set):
        ratio_prev, shift_prev = running
        low_row, main_row, up_row, src_row = row_set
        divisor = main_row - low_row * ratio_prev
        ratio_next = up_row / divisor
        shift_next = (src_row - low_row * shift_prev) / divisor
        return (ratio_next, shift_next), (ratio_next, shift_next)

    zeros_row = jnp.zeros(main_coef.shape[1:], jnp.float32)
    ignored, (ratios, shifts) = lax.scan(forward, (zeros_row, zeros_row), (lower_coef, main_coef, upper_coef, source))

    def backward(after_value, row_set):
        ratio_row, shift_row = row_set
        solved = shift_row - ratio_row * after_value
        return solved, solved

    ignored, solved_rows = lax.scan(backward, zeros_row, (ratios, shifts), reverse=True)
    return solved_rows


def reference(solution_in, residual_in, direction_in, cond_x, cond_y, cond_z, helmholtz):
    low_x = lower_of(cond_x, 1)
    low_y = lower_of(cond_y, 2)
    low_z = lower_of(cond_z, 0)
    diagonal = helmholtz + cond_x + low_x + cond_y + low_y + cond_z + low_z
    coeffs = (cond_x, cond_y, cond_z, low_x, low_y, low_z, diagonal)
    image_old = operate(direction_in, coeffs)
    precond = tridiagonal(-low_z, diagonal, -cond_z, residual_in)
    conj = -jnp.sum(precond * image_old) / jnp.sum(direction_in * image_old)
    direction_out = precond + conj * direction_in
    image = operate(direction_out, coeffs)
    step_size = jnp.sum(residual_in * direction_out) / jnp.sum(direction_out * image)
    return solution_in + step_size * direction_out, residual_in - step_size * image, direction_out
```

```python
import jax
import jax.numpy as jnp
from jax import lax
from jax.experimental import pallas as pl
from jax.experimental.pallas import tpu as pltpu
from jax.sharding import PartitionSpec as P

PARTS = 3
QUARTERS = 4
WIDTH = 128 // QUARTERS
ROWS = 8
BACK = 2
LEFT = 2 * WIDTH
FLUX = LEFT + 1
SUMS = FLUX + WIDTH
VMEM = pl.BlockSpec(memory_space=pltpu.VMEM)
ANY = pl.BlockSpec(memory_space=pl.ANY)


def shape(*dims):
    return jax.ShapeDtypeStruct(dims, jnp.float32)


def shifted(value, axis, by):
    count = lax.axis_size(axis)
    return lax.ppermute(value, axis, [(i, i + by) for i in range(count) if 0 <= i + by < count])


def iota(axis):
    return lax.broadcasted_iota(jnp.int32, (8, 128), axis)


def down(tile, by=1):
    return pltpu.roll(tile, by % 8, 0)


def right(tile, by=1):
    return pltpu.roll(tile, by % 128, 1)


def lane(tile, at):
    return jnp.broadcast_to(tile[:, at:at + 1], (8, 128))


def far(y_got, k, v):
    return lane(y_got[k // 16], k % 16 * 8 + v)


def from_below(up, k, v, to=0):
    at = k * 5 + v
    return down(up[at // 8], to - at % 8)


def partial_diagonal(k, edge, cond_x, cond_y, cond_z, helmholtz):
    row, col = iota(0), iota(1)
    cx, cy = cond_x[k], cond_y[k]
    low_y = jnp.where(col == 0, edge, right(cy))
    low_x = jnp.where(row == 0, 0.0, down(cx))
    total = helmholtz[k] + cx + low_x + cy + low_y + cond_z[k]
    return total + cond_z[k - 1] if k else total


def face_kernel(*refs):
    given, y_face, x_face, held, sems = refs[:6], refs[6], refs[7], refs[8:14], refs[14]
    n = given[0].shape[0]
    copies = [pltpu.make_async_copy(src, dst, sems.at[a]) for a, (src, dst) in enumerate(zip(given, held))]
    for copy in copies:
        copy.start()
    for copy in copies:
        copy.wait()
    dirn, resid, cond_x, cond_y, cond_z, helmholtz = held
    row, col = iota(0), iota(1)
    face = 127 - 127 * lax.axis_index("gy")
    y_tiles = [jnp.zeros((8, 128), jnp.float32) for t in range(y_face.shape[0])]
    x_tiles = [jnp.zeros((8, 128), jnp.float32) for t in range(x_face.shape[0])]
    for k in range(n):
        diag = partial_diagonal(k, 0.0, cond_x, cond_y, cond_z, helmholtz)
        for v, value in enumerate((dirn[k], cond_y[k], diag, cond_z[k], resid[k], cond_x[k])):
            at = k % 16 * 8 + v
            moved = pltpu.roll(value, lax.rem(at - face + 256, 128), 1)
            y_tiles[k // 16] = jnp.where(col == at, moved, y_tiles[k // 16])
        for v, value in enumerate((dirn[k], cond_x[k], diag, cond_z[k], resid[k])):
            at = k * 5 + v
            x_tiles[at // 8] = jnp.where(row == at % 8, down(value, at % 8 - 7), x_tiles[at // 8])
    for ref, tiles in ((y_face, y_tiles), (x_face, x_tiles)):
        for t, tile in enumerate(tiles):
            ref[t] = tile


def condense(main, link, source):
    n = len(main)
    zero = jnp.zeros_like(main[0])
    base, first, last = [zero] * n, [zero + 1.0] + [zero] * (n - 1), [zero] * n
    for k in range(1, n):
        low = link[k - 1]
        inv = 1.0 / (main[k] - low * last[k - 1] if k > 1 else main[k])
        base[k] = (source[k] + low * base[k - 1]) * inv if k > 1 else source[k] * inv
        first[k] = low * first[k - 1] * inv
        last[k] = link[k] * inv
    for k in range(n - 2, 0, -1):
        ratio = last[k]
        base[k] = base[k] + ratio * base[k + 1]
        first[k] = first[k] + ratio * first[k + 1]
        last[k] = ratio * last[k + 1]
    return base, first, last


def ends(main, link, source, parts):
    base, first, last = parts
    return [
        main[0] - link[0] * first[1],
        link[0] * last[1],
        source[0] + link[0] * base[1],
        link[-1] - link[-1] * last[-1],
        link[-1] * base[-1],
    ]


def sides(core, field, below, beside):
    row, col = iota(0), iota(1)
    after = jnp.where(row == 7, 0.0, down(field, -1))
    before = jnp.where(row == 0, below, down(field))
    upper = jnp.where(col == 127, jnp.where(core == 0, beside, 0.0), right(field, -1))
    lower = jnp.where(col == 0, jnp.where(core == 0, 0.0, beside), right(field))
    return after, before, upper, lower


def block_kernel(dirn, resid, cond_x, cond_y, cond_z, helmholtz, y_got, diagonal_got, up,
                 spread, own_parts, ext_parts, far_parts, image, lows):
    core = lax.axis_index("gy")
    row, col = iota(0), iota(1)
    n = dirn.shape[0]
    levels = range(n)
    first_row = lambda a: jnp.where(row == 0, a, 0.0)

    own_m, ext_m, far_m, ext_c, ext_r, far_c, far_r = [], [], [], [], [], [], []
    low_xs, low_ys, sides_d, ext_ds = [], [], [], []
    for k in levels:
        cx, cy = cond_x[k], cond_y[k]
        low_x = jnp.where(row == 0, from_below(up, k, 1), down(cx))
        edge = jnp.where(core == 1, far(y_got, k, 1), 0.0)
        low_y = jnp.where(col == 0, edge, right(cy))
        diag = partial_diagonal(k, edge, cond_x, cond_y, cond_z, helmholtz)
        low_xs.append(low_x)
        low_ys.append(low_y)
        own_m.append(diag + first_row(low_x))
        corner = jnp.where(jnp.logical_and(core == 1, col == 0), down(far(diagonal_got, k, 1), 1), 0.0)
        found = first_row(from_below(up, k, 2) + corner)
        ext_m.append(jnp.where(found > 0.0, found, 1.0))
        ext_c.append(first_row(from_below(up, k, 3)))
        ext_r.append(first_row(from_below(up, k, 4)))
        far_m.append(far(y_got, k, 2) + first_row(down(far(diagonal_got, k, 5), 1))
                     + jnp.where(core == 0, lane(cy, 127), 0.0))
        far_c.append(far(y_got, k, 3))
        far_r.append(far(y_got, k, 4))
        ext_ds.append(first_row(from_below(up, k, 0)))
        after, before, upper, lower = sides(core, dirn[k], ext_ds[k], far(y_got, k, 0))
        sides_d.append(cx * after + low_x * before + cy * upper + low_y * lower)
        lows[0, k] = low_x
        lows[1, k] = low_y

    own_c = [cond_z[k] for k in levels]
    own_r = [resid[k] for k in levels]
    own = condense(own_m, own_c, own_r)
    ext = condense(ext_m, ext_c, ext_r)
    beside = condense(far_m, far_c, far_r)
    for ref, parts in ((own_parts, own), (ext_parts, ext), (far_parts, beside)):
        for v in range(3):
            for k in levels:
                ref[v, k] = parts[v][k]

    zero = jnp.zeros((8, 128), jnp.float32)
    c0 = g0 = g1 = g2 = h0 = h1 = h2 = d_ad = r_d = zero
    below_g1 = below_g2 = below_h1 = below_h2 = zero
    quad_x, quad_y = [zero] * 4, [zero] * 4
    flux = zero
    for k in levels:
        d, cx, cy = dirn[k], cond_x[k], cond_y[k]
        low_x, low_y, side = low_xs[k], low_ys[k], sides_d[k]
        b, f, l = own[0][k], own[1][k], own[2][k]
        eb, ef, el = ext[0][k], ext[1][k], ext[2][k]
        face_d, face_b = first_row(low_x * d), first_row(low_x * b)
        below_g1 = below_g1 + face_d * ef
        below_g2 = below_g2 + face_d * el
        g0 = g0 + face_d * eb
        if k:
            after, before, upper, lower = sides(core, b, eb, beside[0][k])
            side_b = cx * after + low_x * before + cy * upper + low_y * lower
            c0 = c0 + resid[k] * b
            g0 = g0 + side * b
            h0 = h0 + side_b * b + face_b * eb
            h1 = h1 + side_b * f
            h2 = h2 + side_b * l
            g2 = g2 + side * l
            below_h1 = below_h1 + face_b * ef
            below_h2 = below_h2 + face_b * el
        g1 = g1 + side * f
        fx = jnp.where(row == 0, ef, down(f))
        lx = jnp.where(row == 0, el, down(l))
        fy = jnp.where(col == 0, beside[1][k], right(f))
        ly = jnp.where(col == 0, beside[2][k], right(l))
        for quad, cond, f_to, l_to in ((quad_x, low_x, fx, lx), (quad_y, low_y, fy, ly)):
            cf, cl = cond * f, cond * l
            for at, term in enumerate((cf * f_to, cf * l_to, cl * f_to, cl * l_to)):
                quad[at] = quad[at] + term
        local = (helmholtz[k] + cx + low_x + cy + low_y) * d - side
        d_ad = d_ad + d * local - face_d * ext_ds[k]
        r_d = r_d + resid[k] * d
        local = local - flux
        if k + 1 < n:
            gap = d - dirn[k + 1]
            flux = cond_z[k] * gap
            d_ad = d_ad + flux * gap
            local = local + flux
        image[k] = local

    chain = ends(own_m, own_c, own_r, own)
    chain_ext = ends(ext_m, ext_c, ext_r, ext)
    chain_far = ends(far_m, far_c, far_r, beside)
    chain_x = [jnp.where(row == 0, e, down(o)) for o, e in zip(chain, chain_ext)]
    chain_y = [jnp.where(col == 0, e, right(o)) for o, e in zip(chain, chain_far)]
    spot = lax.rem(col, WIDTH)
    left = sums = zero
    for v in range(5):
        left = jnp.where(spot == v, right(chain_y[v], v), left)
    for v, part in enumerate((c0, g0, h0, d_ad, r_d)):
        sums = jnp.where(col == v, jnp.sum(part, axis=1, keepdims=True), sums)
    others = ([2.0 * q for q in quad_x] + [2.0 * q for q in quad_y]
              + [2.0 * h1, 2.0 * h2, g1, g2, 2.0 * below_h1, 2.0 * below_h2, below_g1, below_g2]
              + [dirn[0], dirn[n - 1], cond_z[n - 1], left, sums, zero])
    table = [[chain[v], chain_x[v], others[2 * v], others[2 * v + 1]] for v in range(5)]
    table += [others[at:at + 4] for at in (10, 14, 18)]
    block = lax.div(col, WIDTH)
    for quarter in range(QUARTERS):
        for at, values in enumerate(table):
            tile = zero
            for b, value in enumerate(values):
                tile = jnp.where(block == b, right(value, WIDTH * (b - quarter)), tile)
            spread[pl.ds(quarter * ROWS + at, 8, stride=QUARTERS * ROWS), :] = tile


def row_kernel(back, own_parts, dirn, low):
    row = iota(0)
    tiles = [jnp.zeros((8, 128), jnp.float32) for t in range(low.shape[0])]
    for k in range(dirn.shape[0]):
        for v, value in enumerate((own_parts[0, k], own_parts[1, k], own_parts[2, k], dirn[k])):
            at = k * 4 + v
            tiles[at // 8] = jnp.where(row == at % 8, down(value, at % 8), tiles[at // 8])
    for t, tile in enumerate(tiles):
        low[t] = tile


def solver_kernel(rows, back, mains, links, sources, found):
    n = rows.shape[0] // ROWS
    half = n // 2
    lanes = lax.broadcasted_iota(jnp.int32, (n, 128), 1)
    level = lax.broadcasted_iota(jnp.int32, (n, 128), 0)
    take = lambda at: rows[pl.ds(at, n, stride=ROWS), :]
    shift_to = lambda value, by: pltpu.roll(value, by % 128, 1)
    previous = lambda value: jnp.where(level == 0, 0.0, pltpu.roll(value, 1, 0))
    lines = [take(at) for at in range(ROWS)]

    def other(v):
        at, b = (v // 2, 2 + v % 2) if v < 10 else (5 + (v - 10) // 4, (v - 10) % 4)
        return shift_to(lines[at], -b * WIDTH)

    left = other(19)
    chain = []
    for v in range(5):
        value = jnp.where(lanes == LEFT, shift_to(left, LEFT - v), lines[v])
        chain.append(jnp.where(lanes > LEFT, 1.0 if v == 0 else 0.0, value))
    source = chain[2] + previous(chain[4])
    mains[...] = chain[0] + previous(chain[3])
    links[...] = chain[1]
    sources[...] = source
    main = [mains[j:j + 1, :] for j in range(n)]
    link = [links[j:j + 1, :] for j in range(n)]
    src = [sources[j:j + 1, :] for j in range(n)]
    ratio, shift = [None] * n, [None] * n
    for j in range(half):
        a, b = j, n - 1 - j
        if j:
            inv_a = 1.0 / (main[a] - link[a - 1] * ratio[a - 1])
            inv_b = 1.0 / (main[b] - link[b] * ratio[b + 1])
            shift[a] = (src[a] + link[a - 1] * shift[a - 1]) * inv_a
            shift[b] = (src[b] + link[b] * shift[b + 1]) * inv_b
        else:
            inv_a, inv_b = 1.0 / main[a], 1.0 / main[b]
            shift[a], shift[b] = src[a] * inv_a, src[b] * inv_b
        ratio[a] = link[a] * inv_a
        ratio[b] = link[b - 1] * inv_b
    x = [None] * n
    a, b = half - 1, half
    x[a] = (shift[a] + ratio[a] * shift[b]) / (1.0 - ratio[a] * ratio[b])
    x[b] = shift[b] + ratio[b] * x[a]
    for j in range(half - 2, -1, -1):
        x[j] = shift[j] + ratio[j] * x[j + 1]
        m = n - 1 - j
        x[m] = shift[m] + ratio[m] * x[m - 1]
    for j in range(n):
        found[j:j + 1, :] = x[j]

    x = found[...]
    x2 = jnp.where(level == n - 1, 0.0, pltpu.roll(x, n - 1, 0))
    below, below2 = shift_to(x, -WIDTH), shift_to(x2, -WIDTH)
    beside = jnp.where(lanes == 0, shift_to(x, -LEFT), shift_to(x, 1))
    beside2 = jnp.where(lanes == 0, shift_to(x2, -LEFT), shift_to(x2, 1))
    quad = (x * (other(0) * below + other(1) * below2 + other(4) * beside + other(5) * beside2)
            + x2 * (other(2) * below + other(3) * below2 + other(6) * beside + other(7) * beside2))
    sum_h = quad + x * other(8) + x2 * other(9) + below * other(12) + below2 * other(13)
    sum_g = x * other(10) + x2 * other(11) + below * other(14) + below2 * other(15)
    gap = other(17) - jnp.where(level == n - 1, 0.0, pltpu.roll(other(16), n - 1, 0))
    flux = other(18) * gap
    amounts = [x * source, sum_g, sum_h, flux * gap, None]
    known = jnp.sum(other(20), axis=0, keepdims=True)
    lane_row = lax.broadcasted_iota(jnp.int32, (1, 128), 1)
    scalars = jnp.where(lane_row < 5, known, 0.0)
    for v, amount in enumerate(amounts[:4]):
        amount = jnp.where(lane_row < WIDTH, jnp.sum(amount, axis=0, keepdims=True), 0.0)
        scalars = scalars + jnp.where(lane_row == v, jnp.sum(amount, axis=1, keepdims=True), 0.0)
    scalars = jnp.broadcast_to(pltpu.roll(jnp.broadcast_to(scalars, (8, 128)), SUMS, 1)[0:1, :], (n, 128))
    in_flux = jnp.logical_and(lanes >= FLUX, lanes < SUMS)
    tail = jnp.where(lanes >= SUMS, scalars, 0.0)
    back[pl.ds(0, n, stride=BACK), :] = jnp.where(
        lanes <= LEFT, x, jnp.where(in_flux, shift_to(previous(flux), FLUX), tail))
    back[pl.ds(1, n, stride=BACK), :] = jnp.where(lanes <= LEFT, x2, jnp.where(in_flux, shift_to(flux, FLUX), tail))


def scalar_kernel(tops, got, spread):
    n = got.shape[0] // BACK
    amount = jnp.sum(got[pl.ds(0, n, stride=BACK), :], axis=0, keepdims=True)
    for t in range(0, spread.shape[0], 3):
        spread[t] = amount
        spread[t + 1] = tops[0:1, :]
        spread[t + 2] = tops[1:2, :]


def column_kernel(low, got, resid, cond_x, cond_y, own_parts, ext_parts, far_parts, image_in, lows,
                  precond, image_p, image_d, tops):
    core = lax.axis_index("gy")
    n = resid.shape[0]
    block = lax.div(iota(1), WIDTH)
    part = lambda quarter, v: got[pl.ds(quarter * BACK + v, 8, stride=QUARTERS * BACK), :]

    def gather(v, lane_from):
        tile = jnp.zeros((8, 128), jnp.float32)
        for quarter in range(QUARTERS):
            tile = jnp.where(block == quarter, right(part(quarter, v), WIDTH * quarter - lane_from), tile)
        return tile

    x, x2 = gather(0, 0), gather(1, 0)
    ext_x, ext_x2 = gather(0, WIDTH), gather(1, WIDTH)
    far_x, far_x2 = lane(part(0, 0), LEFT), lane(part(0, 1), LEFT)
    flux_below, flux_above = gather(0, FLUX), gather(1, FLUX)
    tops[...] = jnp.where(iota(0) == 0, x, down(x2))
    join = lambda parts, k, a, b: parts[0, k] + a * parts[1, k] + b * parts[2, k]
    for k in range(n):
        p = join(own_parts, k, x, x2)
        ext = join(ext_parts, k, ext_x, ext_x2)
        beside = join(far_parts, k, far_x, far_x2)
        after, before, upper, lower = sides(core, p, ext, beside)
        side = cond_x[k] * after + lows[0, k] * before + cond_y[k] * upper + lows[1, k] * lower
        precond[k] = p
        image_p[k] = resid[k] - side
        local = image_in[k]
        if k == 0:
            local = local - flux_below
        if k == n - 1:
            local = local + flux_above
        image_d[k] = local


def update_kernel(scalars, low, cond_x, sol, resid, dirn, precond, image_p, image_d,
                  sol_to, res_to, dir_to, sol_out, res_out, dir_out, sems):
    row = iota(0)
    mates = scalars.shape[0] // 3
    amount = scalars[0]
    for t in range(1, mates):
        amount = amount + scalars[3 * t]
    per_row = lax.axis_size("gy")
    mate = lax.axis_index("gx") * per_row + lax.axis_index("gy") + per_row
    mate = jnp.minimum(mate, mates - 1)
    x, x2 = (jnp.broadcast_to(scalars[3 * mate + v], (8, 128)) for v in (1, 2))
    r_p, p_nd, p_np, d_ad, r_d = (jnp.broadcast_to(amount[:, v:v + 1], (8, 128)) for v in range(SUMS, SUMS + 5))
    p_ad = r_d - p_nd
    conj = -p_ad / d_ad
    step = (r_p + conj * r_d) / (r_p - p_np + conj * p_ad)
    n = sol.shape[0]
    size = n // PARTS
    copies = []
    for k in range(n):
        out = precond[k] + conj * dirn[k]
        dir_out[k] = out
        sol_out[k] = sol[k] + step * out
        b_up, f_up, l_up, d_up = (down(low[(4 * k + v) // 8], 7 - (4 * k + v) % 8) for v in range(4))
        p_up = b_up + x * f_up + x2 * l_up
        above = jnp.where(row == 7, cond_x[k] * (p_up + conj * d_up), 0.0)
        res_out[k] = resid[k] - step * (image_p[k] + conj * image_d[k] - above)
        if (k + 1) % size == 0:
            part = k // size
            levels = pl.ds(part * size, size)
            for a, (src, dst) in enumerate(((sol_out, sol_to), (res_out, res_to), (dir_out, dir_to))):
                copies.append(pltpu.make_async_copy(src.at[levels], dst.at[levels], sems.at[3 * part + a]))
                copies[-1].start()
    for copy in copies:
        copy.wait()


def call(kernel, outs, *args, scratch=(), first=0, out_spec=VMEM):
    many = isinstance(outs, tuple)
    return pl.pallas_call(
        kernel, out_shape=outs, in_specs=[ANY] * first + [VMEM] * (len(args) - first),
        out_specs=(out_spec,) * len(outs) if many else out_spec, scratch_shapes=scratch,
        compiler_params=pltpu.CompilerParams(vmem_limit_bytes=8 << 20))(*args)


def body(solution_in, residual_in, direction_in, cond_x, cond_y, cond_z, helmholtz):
    nz, nx, ny = direction_in.shape
    gz, gx = lax.axis_size("gz"), lax.axis_size("gx")
    mates = gx * lax.axis_size("gy")
    field = shape(nz, nx, ny)
    parts = shape(3, nz, nx, ny)
    given = [pltpu.with_memory_space_constraint(a, pltpu.HBM)
             for a in (direction_in, residual_in, cond_x, cond_y, cond_z, helmholtz)]

    y_face, x_face, *given = call(
        face_kernel, (shape(-(-nz // 16), nx, ny), shape(nz * 5 // 8, nx, ny)) + (field,) * 6, *given,
        scratch=(pltpu.SemaphoreType.DMA((6,)),), first=6)
    direction_in, residual_in, cond_x, cond_y, cond_z, helmholtz = given
    up = shifted(x_face, "gx", 1)
    y_got = lax.ppermute(y_face, "gy", [(0, 1), (1, 0)])
    diagonal_got = lax.ppermute(y_face, ("gx", "gy"), [
        (2 * i + c, 2 * i + 3 - c) for i in range(gx - 1) for c in range(2)])
    spread, own_parts, ext_parts, far_parts, image, lows = call(
        block_kernel, (shape(gz * ROWS, ny), parts, parts, parts, field, shape(2, nz, nx, ny)),
        *given, y_got, diagonal_got, up)
    rows = lax.all_to_all(spread.reshape(gz, ROWS, ny), "gz", 0, 0, tiled=True)
    back = call(solver_kernel, shape(gz * BACK, ny), rows.reshape(gz * ROWS, ny),
                scratch=(pltpu.VMEM((gz, ny), jnp.float32),) * 4)
    low = call(row_kernel, shape(nz // 2, nx, ny), back, own_parts, direction_in, first=1)
    low = shifted(low, "gx", -1)
    got = lax.all_to_all(back.reshape(gz, BACK, ny), "gz", 0, 0, tiled=True).reshape(gz * BACK, ny)
    precond, image_p, image_d, tops = call(
        column_kernel, (field, field, field, shape(8, ny)), low, got, residual_in, cond_x, cond_y,
        own_parts, ext_parts, far_parts, image, lows, first=1)
    sums = call(scalar_kernel, shape(mates * 3, 1, ny), tops, got)
    sums = lax.all_to_all(sums, ("gx", "gy"), 0, 0, tiled=True)
    return call(update_kernel, (field, field, field), sums, low, cond_x, solution_in, residual_in, direction_in,
                precond, image_p, image_d, out_spec=ANY,
                scratch=(pltpu.VMEM((nz, nx, ny), jnp.float32),) * 3 + (pltpu.SemaphoreType.DMA((3 * PARTS,)),))


def solution(mesh):
    spec = P("gz", "gx", "gy")
    return jax.shard_map(body, mesh=mesh, in_specs=(spec,) * 7, out_specs=(spec,) * 3, check_vma=False)
```

```python
import jax
import jax.numpy as jnp
from jax import lax
from jax.experimental import pallas as pl
from jax.experimental.pallas import tpu as pltpu
from jax.sharding import PartitionSpec as P

PARTS = 3
QUARTERS = 4
WIDTH = 128 // QUARTERS
ROWS = 8
BACK = 2
LEFT = 2 * WIDTH
FLUX = LEFT + 1
SUMS = FLUX + WIDTH
VMEM = pl.BlockSpec(memory_space=pltpu.VMEM)
ANY = pl.BlockSpec(memory_space=pl.ANY)


def shape(*dims):
    return jax.ShapeDtypeStruct(dims, jnp.float32)


def shifted(value, axis, by):
    count = lax.axis_size(axis)
    return lax.ppermute(value, axis, [(i, i + by) for i in range(count) if 0 <= i + by < count])


def iota(axis):
    return lax.broadcasted_iota(jnp.int32, (8, 128), axis)


def down(tile, by=1):
    return pltpu.roll(tile, by % 8, 0)


def right(tile, by=1):
    return pltpu.roll(tile, by % 128, 1)


def lane(tile, at):
    return jnp.broadcast_to(tile[:, at:at + 1], (8, 128))


def far(y_got, k, v):
    return lane(y_got[k // 16], k % 16 * 8 + v)


def from_below(up, k, v, to=0):
    at = k * 5 + v
    return down(up[at // 8], to - at % 8)


def partial_diagonal(k, edge, cond_x, cond_y, cond_z, helmholtz):
    row, col = iota(0), iota(1)
    cx, cy = cond_x[k], cond_y[k]
    low_y = jnp.where(col == 0, edge, right(cy))
    low_x = jnp.where(row == 0, 0.0, down(cx))
    total = helmholtz[k] + cx + low_x + cy + low_y + cond_z[k]
    return total + cond_z[k - 1] if k else total


def face_kernel(*refs):
    given, y_face, x_face, held, sems = refs[:6], refs[6], refs[7], refs[8:14], refs[14]
    n = given[0].shape[0]
    size = n // PARTS
    copies = []
    for part in range(PARTS):
        levels = pl.ds(part * size, size)
        for a, (src, dst) in enumerate(zip(given, held)):
            copies.append(pltpu.make_async_copy(src.at[levels], dst.at[levels], sems.at[6 * part + a]))
            copies[-1].start()
    dirn, resid, cond_x, cond_y, cond_z, helmholtz = held
    row, col = iota(0), iota(1)
    face = 127 - 127 * lax.axis_index("gy")
    y_tiles = [jnp.zeros((8, 128), jnp.float32) for t in range(y_face.shape[0])]
    x_tiles = [jnp.zeros((8, 128), jnp.float32) for t in range(x_face.shape[0])]
    for k in range(n):
        if k % size == 0:
            for copy in copies[6 * (k // size):6 * (k // size) + 6]:
                copy.wait()
        diag = partial_diagonal(k, 0.0, cond_x, cond_y, cond_z, helmholtz)
        for v, value in enumerate((dirn[k], cond_y[k], diag, cond_z[k], resid[k], cond_x[k])):
            at = k % 16 * 8 + v
            moved = pltpu.roll(value, lax.rem(at - face + 256, 128), 1)
            y_tiles[k // 16] = jnp.where(col == at, moved, y_tiles[k // 16])
        for v, value in enumerate((dirn[k], cond_x[k], diag, cond_z[k], resid[k])):
            at = k * 5 + v
            x_tiles[at // 8] = jnp.where(row == at % 8, down(value, at % 8 - 7), x_tiles[at // 8])
    for ref, tiles in ((y_face, y_tiles), (x_face, x_tiles)):
        for t, tile in enumerate(tiles):
            ref[t] = tile


def condense(main, link, source):
    n = len(main)
    zero = jnp.zeros_like(main[0])
    base, first, last = [zero] * n, [zero + 1.0] + [zero] * (n - 1), [zero] * n
    for k in range(1, n):
        low = link[k - 1]
        inv = 1.0 / (main[k] - low * last[k - 1] if k > 1 else main[k])
        base[k] = (source[k] + low * base[k - 1]) * inv if k > 1 else source[k] * inv
        first[k] = low * first[k - 1] * inv
        last[k] = link[k] * inv
    for k in range(n - 2, 0, -1):
        ratio = last[k]
        base[k] = base[k] + ratio * base[k + 1]
        first[k] = first[k] + ratio * first[k + 1]
        last[k] = ratio * last[k + 1]
    return base, first, last


def ends(main, link, source, parts):
    base, first, last = parts
    return [
        main[0] - link[0] * first[1],
        link[0] * last[1],
        source[0] + link[0] * base[1],
        link[-1] - link[-1] * last[-1],
        link[-1] * base[-1],
    ]


def sides(core, field, below, beside):
    row, col = iota(0), iota(1)
    after = jnp.where(row == 7, 0.0, down(field, -1))
    before = jnp.where(row == 0, below, down(field))
    upper = jnp.where(col == 127, jnp.where(core == 0, beside, 0.0), right(field, -1))
    lower = jnp.where(col == 0, jnp.where(core == 0, 0.0, beside), right(field))
    return after, before, upper, lower


def block_kernel(dirn, resid, cond_x, cond_y, cond_z, helmholtz, y_got, diagonal_got, up,
                 spread, own_parts, ext_parts, far_parts, image, lows):
    core = lax.axis_index("gy")
    row, col = iota(0), iota(1)
    n = dirn.shape[0]
    levels = range(n)
    first_row = lambda a: jnp.where(row == 0, a, 0.0)

    own_m, ext_m, far_m, ext_c, ext_r, far_c, far_r = [], [], [], [], [], [], []
    low_xs, low_ys, sides_d, ext_ds = [], [], [], []
    for k in levels:
        cx, cy = cond_x[k], cond_y[k]
        low_x = jnp.where(row == 0, from_below(up, k, 1), down(cx))
        edge = jnp.where(core == 1, far(y_got, k, 1), 0.0)
        low_y = jnp.where(col == 0, edge, right(cy))
        diag = partial_diagonal(k, edge, cond_x, cond_y, cond_z, helmholtz)
        low_xs.append(low_x)
        low_ys.append(low_y)
        own_m.append(diag + first_row(low_x))
        corner = jnp.where(jnp.logical_and(core == 1, col == 0), down(far(diagonal_got, k, 1), 1), 0.0)
        found = first_row(from_below(up, k, 2) + corner)
        ext_m.append(jnp.where(found > 0.0, found, 1.0))
        ext_c.append(first_row(from_below(up, k, 3)))
        ext_r.append(first_row(from_below(up, k, 4)))
        far_m.append(far(y_got, k, 2) + first_row(down(far(diagonal_got, k, 5), 1))
                     + jnp.where(core == 0, lane(cy, 127), 0.0))
        far_c.append(far(y_got, k, 3))
        far_r.append(far(y_got, k, 4))
        ext_ds.append(first_row(from_below(up, k, 0)))
        after, before, upper, lower = sides(core, dirn[k], ext_ds[k], far(y_got, k, 0))
        sides_d.append(cx * after + low_x * before + cy * upper + low_y * lower)
        lows[0, k] = low_x
        lows[1, k] = low_y

    own_c = [cond_z[k] for k in levels]
    own_r = [resid[k] for k in levels]
    own = condense(own_m, own_c, own_r)
    ext = condense(ext_m, ext_c, ext_r)
    beside = condense(far_m, far_c, far_r)
    for ref, parts in ((own_parts, own), (ext_parts, ext), (far_parts, beside)):
        for v in range(3):
            for k in levels:
                ref[v, k] = parts[v][k]

    zero = jnp.zeros((8, 128), jnp.float32)
    c0 = g0 = g1 = g2 = h0 = h1 = h2 = d_ad = r_d = zero
    below_g1 = below_g2 = below_h1 = below_h2 = zero
    quad_x, quad_y = [zero] * 4, [zero] * 4
    flux = zero
    for k in levels:
        d, cx, cy = dirn[k], cond_x[k], cond_y[k]
        low_x, low_y, side = low_xs[k], low_ys[k], sides_d[k]
        b, f, l = own[0][k], own[1][k], own[2][k]
        eb, ef, el = ext[0][k], ext[1][k], ext[2][k]
        face_d, face_b = first_row(low_x * d), first_row(low_x * b)
        below_g1 = below_g1 + face_d * ef
        below_g2 = below_g2 + face_d * el
        g0 = g0 + face_d * eb
        if k:
            after, before, upper, lower = sides(core, b, eb, beside[0][k])
            side_b = cx * after + low_x * before + cy * upper + low_y * lower
            c0 = c0 + resid[k] * b
            g0 = g0 + side * b
            h0 = h0 + side_b * b + face_b * eb
            h1 = h1 + side_b * f
            h2 = h2 + side_b * l
            g2 = g2 + side * l
            below_h1 = below_h1 + face_b * ef
            below_h2 = below_h2 + face_b * el
        g1 = g1 + side * f
        fx = jnp.where(row == 0, ef, down(f))
        lx = jnp.where(row == 0, el, down(l))
        fy = jnp.where(col == 0, beside[1][k], right(f))
        ly = jnp.where(col == 0, beside[2][k], right(l))
        for quad, cond, f_to, l_to in ((quad_x, low_x, fx, lx), (quad_y, low_y, fy, ly)):
            cf, cl = cond * f, cond * l
            for at, term in enumerate((cf * f_to, cf * l_to, cl * f_to, cl * l_to)):
                quad[at] = quad[at] + term
        local = (helmholtz[k] + cx + low_x + cy + low_y) * d - side
        d_ad = d_ad + d * local - face_d * ext_ds[k]
        r_d = r_d + resid[k] * d
        local = local - flux
        if k + 1 < n:
            gap = d - dirn[k + 1]
            flux = cond_z[k] * gap
            d_ad = d_ad + flux * gap
            local = local + flux
        image[k] = local

    chain = ends(own_m, own_c, own_r, own)
    chain_ext = ends(ext_m, ext_c, ext_r, ext)
    chain_far = ends(far_m, far_c, far_r, beside)
    chain_x = [jnp.where(row == 0, e, down(o)) for o, e in zip(chain, chain_ext)]
    chain_y = [jnp.where(col == 0, e, right(o)) for o, e in zip(chain, chain_far)]
    spot = lax.rem(col, WIDTH)
    left = sums = zero
    for v in range(5):
        left = jnp.where(spot == v, right(chain_y[v], v), left)
    for v, part in enumerate((c0, g0, h0, d_ad, r_d)):
        sums = jnp.where(col == v, jnp.sum(part, axis=1, keepdims=True), sums)
    others = ([2.0 * q for q in quad_x] + [2.0 * q for q in quad_y]
              + [2.0 * h1, 2.0 * h2, g1, g2, 2.0 * below_h1, 2.0 * below_h2, below_g1, below_g2]
              + [dirn[0], dirn[n - 1], cond_z[n - 1], left, sums, zero])
    table = [[chain[v], chain_x[v], others[2 * v], others[2 * v + 1]] for v in range(5)]
    table += [others[at:at + 4] for at in (10, 14, 18)]
    block = lax.div(col, WIDTH)
    for quarter in range(QUARTERS):
        for at, values in enumerate(table):
            tile = zero
            for b, value in enumerate(values):
                tile = jnp.where(block == b, right(value, WIDTH * (b - quarter)), tile)
            spread[pl.ds(quarter * ROWS + at, 8, stride=QUARTERS * ROWS), :] = tile


def row_kernel(back, own_parts, dirn, low):
    row = iota(0)
    tiles = [jnp.zeros((8, 128), jnp.float32) for t in range(low.shape[0])]
    for k in range(dirn.shape[0]):
        for v, value in enumerate((own_parts[0, k], own_parts[1, k], own_parts[2, k], dirn[k])):
            at = k * 4 + v
            tiles[at // 8] = jnp.where(row == at % 8, down(value, at % 8), tiles[at // 8])
    for t, tile in enumerate(tiles):
        low[t] = tile


def solver_kernel(rows, back, mains, links, sources, found):
    n = rows.shape[0] // ROWS
    half = n // 2
    lanes = lax.broadcasted_iota(jnp.int32, (n, 128), 1)
    level = lax.broadcasted_iota(jnp.int32, (n, 128), 0)
    take = lambda at: rows[pl.ds(at, n, stride=ROWS), :]
    shift_to = lambda value, by: pltpu.roll(value, by % 128, 1)
    previous = lambda value: jnp.where(level == 0, 0.0, pltpu.roll(value, 1, 0))
    lines = [take(at) for at in range(ROWS)]

    def other(v):
        at, b = (v // 2, 2 + v % 2) if v < 10 else (5 + (v - 10) // 4, (v - 10) % 4)
        return shift_to(lines[at], -b * WIDTH)

    left = other(19)
    chain = []
    for v in range(5):
        value = jnp.where(lanes == LEFT, shift_to(left, LEFT - v), lines[v])
        chain.append(jnp.where(lanes > LEFT, 1.0 if v == 0 else 0.0, value))
    source = chain[2] + previous(chain[4])
    mains[...] = chain[0] + previous(chain[3])
    links[...] = chain[1]
    sources[...] = source
    main = [mains[j:j + 1, :] for j in range(n)]
    link = [links[j:j + 1, :] for j in range(n)]
    src = [sources[j:j + 1, :] for j in range(n)]
    ratio, shift = [None] * n, [None] * n
    for j in range(half):
        a, b = j, n - 1 - j
        if j:
            inv_a = 1.0 / (main[a] - link[a - 1] * ratio[a - 1])
            inv_b = 1.0 / (main[b] - link[b] * ratio[b + 1])
            shift[a] = (src[a] + link[a - 1] * shift[a - 1]) * inv_a
            shift[b] = (src[b] + link[b] * shift[b + 1]) * inv_b
        else:
            inv_a, inv_b = 1.0 / main[a], 1.0 / main[b]
            shift[a], shift[b] = src[a] * inv_a, src[b] * inv_b
        ratio[a] = link[a] * inv_a
        ratio[b] = link[b - 1] * inv_b
    x = [None] * n
    a, b = half - 1, half
    x[a] = (shift[a] + ratio[a] * shift[b]) / (1.0 - ratio[a] * ratio[b])
    x[b] = shift[b] + ratio[b] * x[a]
    for j in range(half - 2, -1, -1):
        x[j] = shift[j] + ratio[j] * x[j + 1]
        m = n - 1 - j
        x[m] = shift[m] + ratio[m] * x[m - 1]
    for j in range(n):
        found[j:j + 1, :] = x[j]

    x = found[...]
    x2 = jnp.where(level == n - 1, 0.0, pltpu.roll(x, n - 1, 0))
    below, below2 = shift_to(x, -WIDTH), shift_to(x2, -WIDTH)
    beside = jnp.where(lanes == 0, shift_to(x, -LEFT), shift_to(x, 1))
    beside2 = jnp.where(lanes == 0, shift_to(x2, -LEFT), shift_to(x2, 1))
    quad = (x * (other(0) * below + other(1) * below2 + other(4) * beside + other(5) * beside2)
            + x2 * (other(2) * below + other(3) * below2 + other(6) * beside + other(7) * beside2))
    sum_h = quad + x * other(8) + x2 * other(9) + below * other(12) + below2 * other(13)
    sum_g = x * other(10) + x2 * other(11) + below * other(14) + below2 * other(15)
    gap = other(17) - jnp.where(level == n - 1, 0.0, pltpu.roll(other(16), n - 1, 0))
    flux = other(18) * gap
    amounts = [x * source, sum_g, sum_h, flux * gap, None]
    known = jnp.sum(other(20), axis=0, keepdims=True)
    lane_row = lax.broadcasted_iota(jnp.int32, (1, 128), 1)
    scalars = jnp.where(lane_row < 5, known, 0.0)
    for v, amount in enumerate(amounts[:4]):
        amount = jnp.where(lane_row < WIDTH, jnp.sum(amount, axis=0, keepdims=True), 0.0)
        scalars = scalars + jnp.where(lane_row == v, jnp.sum(amount, axis=1, keepdims=True), 0.0)
    scalars = jnp.broadcast_to(pltpu.roll(jnp.broadcast_to(scalars, (8, 128)), SUMS, 1)[0:1, :], (n, 128))
    in_flux = jnp.logical_and(lanes >= FLUX, lanes < SUMS)
    tail = jnp.where(lanes >= SUMS, scalars, 0.0)
    back[pl.ds(0, n, stride=BACK), :] = jnp.where(
        lanes <= LEFT, x, jnp.where(in_flux, shift_to(previous(flux), FLUX), tail))
    back[pl.ds(1, n, stride=BACK), :] = jnp.where(lanes <= LEFT, x2, jnp.where(in_flux, shift_to(flux, FLUX), tail))


def scalar_kernel(low, tops, got, spread):
    n = got.shape[0] // BACK
    amount = jnp.sum(got[pl.ds(0, n, stride=BACK), :], axis=0, keepdims=True)
    for t in range(spread.shape[0]):
        spread[t, 0:1, :] = amount
        spread[t, 1:3, :] = tops[0:2, :]
        spread[t, 3:4, :] = amount


def column_kernel(got, resid, cond_x, cond_y, own_parts, ext_parts, far_parts, image_in, lows,
                  precond, image_p, image_d, tops):
    core = lax.axis_index("gy")
    n = resid.shape[0]
    block = lax.div(iota(1), WIDTH)
    part = lambda quarter, v: got[pl.ds(quarter * BACK + v, 8, stride=QUARTERS * BACK), :]

    def gather(v, lane_from):
        tile = jnp.zeros((8, 128), jnp.float32)
        for quarter in range(QUARTERS):
            tile = jnp.where(block == quarter, right(part(quarter, v), WIDTH * quarter - lane_from), tile)
        return tile

    x, x2 = gather(0, 0), gather(1, 0)
    ext_x, ext_x2 = gather(0, WIDTH), gather(1, WIDTH)
    far_x, far_x2 = lane(part(0, 0), LEFT), lane(part(0, 1), LEFT)
    flux_below, flux_above = gather(0, FLUX), gather(1, FLUX)
    tops[...] = jnp.where(iota(0) == 0, x, down(x2))
    join = lambda parts, k, a, b: parts[0, k] + a * parts[1, k] + b * parts[2, k]
    for k in range(n):
        p = join(own_parts, k, x, x2)
        ext = join(ext_parts, k, ext_x, ext_x2)
        beside = join(far_parts, k, far_x, far_x2)
        after, before, upper, lower = sides(core, p, ext, beside)
        side = cond_x[k] * after + lows[0, k] * before + cond_y[k] * upper + lows[1, k] * lower
        precond[k] = p
        image_p[k] = resid[k] - side
        local = image_in[k]
        if k == 0:
            local = local - flux_below
        if k == n - 1:
            local = local + flux_above
        image_d[k] = local


def update_kernel(scalars, low, cond_x, sol, resid, dirn, precond, image_p, image_d,
                  sol_out, res_out, dir_out):
    row = iota(0)
    amount = jnp.sum(scalars[:, 0, :], axis=0, keepdims=True)
    per_row = lax.axis_size("gy")
    mate = lax.axis_index("gx") * per_row + lax.axis_index("gy") + per_row
    mate = jnp.minimum(mate, scalars.shape[0] - 1)
    x, x2 = (jnp.broadcast_to(scalars[mate, v:v + 1, :], (8, 128)) for v in (1, 2))
    r_p, p_nd, p_np, d_ad, r_d = (jnp.broadcast_to(amount[:, v:v + 1], (8, 128)) for v in range(SUMS, SUMS + 5))
    p_ad = r_d - p_nd
    conj = -p_ad / d_ad
    step = (r_p + conj * r_d) / (r_p - p_np + conj * p_ad)
    for k in range(sol.shape[0]):
        out = precond[k] + conj * dirn[k]
        dir_out[k] = out
        sol_out[k] = sol[k] + step * out
        b_up, f_up, l_up, d_up = (down(low[(4 * k + v) // 8], 7 - (4 * k + v) % 8) for v in range(4))
        p_up = b_up + x * f_up + x2 * l_up
        above = jnp.where(row == 7, cond_x[k] * (p_up + conj * d_up), 0.0)
        res_out[k] = resid[k] - step * (image_p[k] + conj * image_d[k] - above)


def call(kernel, outs, *args, scratch=(), first=0):
    many = isinstance(outs, tuple)
    return pl.pallas_call(
        kernel, out_shape=outs, in_specs=[ANY] * first + [VMEM] * (len(args) - first),
        out_specs=(VMEM,) * len(outs) if many else VMEM, scratch_shapes=scratch,
        compiler_params=pltpu.CompilerParams(vmem_limit_bytes=8 << 20))(*args)


def body(solution_in, residual_in, direction_in, cond_x, cond_y, cond_z, helmholtz):
    nz, nx, ny = direction_in.shape
    gz, gx = lax.axis_size("gz"), lax.axis_size("gx")
    mates = gx * lax.axis_size("gy")
    field = shape(nz, nx, ny)
    parts = shape(3, nz, nx, ny)
    given = [pltpu.with_memory_space_constraint(a, pltpu.HBM)
             for a in (direction_in, residual_in, cond_x, cond_y, cond_z, helmholtz)]

    y_face, x_face, *given = call(
        face_kernel, (shape(-(-nz // 16), nx, ny), shape(nz * 5 // 8, nx, ny)) + (field,) * 6, *given,
        scratch=(pltpu.SemaphoreType.DMA((6 * PARTS,)),), first=6)
    direction_in, residual_in, cond_x, cond_y, cond_z, helmholtz = given
    up = shifted(x_face, "gx", 1)
    y_got = lax.ppermute(y_face, "gy", [(0, 1), (1, 0)])
    diagonal_got = lax.ppermute(y_face, ("gx", "gy"), [
        (2 * i + c, 2 * i + 3 - c) for i in range(gx - 1) for c in range(2)])
    spread, own_parts, ext_parts, far_parts, image, lows = call(
        block_kernel, (shape(gz * ROWS, ny), parts, parts, parts, field, shape(2, nz, nx, ny)),
        *given, y_got, diagonal_got, up)
    rows = lax.all_to_all(spread.reshape(gz, ROWS, ny), "gz", 0, 0, tiled=True)
    back = call(solver_kernel, shape(gz * BACK, ny), rows.reshape(gz * ROWS, ny),
                scratch=(pltpu.VMEM((gz, ny), jnp.float32),) * 4)
    low = call(row_kernel, shape(nz // 2, nx, ny), back, own_parts, direction_in, first=1)
    low = shifted(low, "gx", -1)
    got = lax.all_to_all(back.reshape(gz, BACK, ny), "gz", 0, 0, tiled=True).reshape(gz * BACK, ny)
    precond, image_p, image_d, tops = call(
        column_kernel, (field, field, field, shape(8, ny)), got, residual_in, cond_x, cond_y,
        own_parts, ext_parts, far_parts, image, lows)
    sums = call(scalar_kernel, shape(mates, 4, ny), low, tops, got, first=1)
    sums = lax.all_to_all(sums, ("gx", "gy"), 0, 0, tiled=True)
    return call(update_kernel, (field, field, field), sums, low, cond_x, solution_in, residual_in, direction_in,
                precond, image_p, image_d)


def solution(mesh):
    spec = P("gz", "gx", "gy")
    return jax.shard_map(body, mesh=mesh, in_specs=(spec,) * 7, out_specs=(spec,) * 3, check_vma=False)
```

```python
import jax
import jax.numpy as jnp
from jax import lax
from jax.experimental import pallas as pl
from jax.experimental.pallas import tpu as pltpu
from jax.sharding import PartitionSpec as P

PARTS = 2
QUARTERS = 4
WIDTH = 128 // QUARTERS
ROWS = 8
BACK = 2
LEFT = 2 * WIDTH
FLUX = LEFT + 1
SUMS = FLUX + WIDTH
VMEM = pl.BlockSpec(memory_space=pltpu.VMEM)
ANY = pl.BlockSpec(memory_space=pl.ANY)


def shape(*dims):
    return jax.ShapeDtypeStruct(dims, jnp.float32)


def shifted(value, axis, by):
    count = lax.axis_size(axis)
    return lax.ppermute(value, axis, [(i, i + by) for i in range(count) if 0 <= i + by < count])


def iota(axis):
    return lax.broadcasted_iota(jnp.int32, (8, 128), axis)


def down(tile, by=1):
    return pltpu.roll(tile, by % 8, 0)


def right(tile, by=1):
    return pltpu.roll(tile, by % 128, 1)


def lane(tile, at):
    return jnp.broadcast_to(tile[:, at:at + 1], (8, 128))


def far(y_got, k, v):
    return lane(y_got[k // 16], k % 16 * 8 + v)


def from_below(up, k, v, to=0):
    at = k * 5 + v
    return down(up[at // 8], to - at % 8)


def partial_diagonal(k, edge, cond_x, cond_y, cond_z, helmholtz):
    row, col = iota(0), iota(1)
    cx, cy = cond_x[k], cond_y[k]
    low_y = jnp.where(col == 0, edge, right(cy))
    low_x = jnp.where(row == 0, 0.0, down(cx))
    total = helmholtz[k] + cx + low_x + cy + low_y + cond_z[k]
    return total + cond_z[k - 1] if k else total


def face_kernel(*refs):
    given, y_face, x_face, held, sems = refs[:6], refs[6], refs[7], refs[8:14], refs[14]
    n = given[0].shape[0]
    size = n // PARTS
    copies = []
    for part in range(PARTS):
        levels = pl.ds(part * size, size)
        for a, (src, dst) in enumerate(zip(given, held)):
            copies.append(pltpu.make_async_copy(src.at[levels], dst.at[levels], sems.at[6 * part + a]))
            copies[-1].start()
    dirn, resid, cond_x, cond_y, cond_z, helmholtz = held
    row, col = iota(0), iota(1)
    face = 127 - 127 * lax.axis_index("gy")
    y_tiles = [jnp.zeros((8, 128), jnp.float32) for t in range(y_face.shape[0])]
    x_tiles = [jnp.zeros((8, 128), jnp.float32) for t in range(x_face.shape[0])]
    for k in range(n):
        if k % size == 0:
            for copy in copies[6 * (k // size):6 * (k // size) + 6]:
                copy.wait()
        diag = partial_diagonal(k, 0.0, cond_x, cond_y, cond_z, helmholtz)
        for v, value in enumerate((dirn[k], cond_y[k], diag, cond_z[k], resid[k], cond_x[k])):
            at = k % 16 * 8 + v
            moved = pltpu.roll(value, lax.rem(at - face + 256, 128), 1)
            y_tiles[k // 16] = jnp.where(col == at, moved, y_tiles[k // 16])
        for v, value in enumerate((dirn[k], cond_x[k], diag, cond_z[k], resid[k])):
            at = k * 5 + v
            x_tiles[at // 8] = jnp.where(row == at % 8, down(value, at % 8 - 7), x_tiles[at // 8])
    for ref, tiles in ((y_face, y_tiles), (x_face, x_tiles)):
        for t, tile in enumerate(tiles):
            ref[t] = tile


def condense(main, link, source):
    n = len(main)
    zero = jnp.zeros_like(main[0])
    base, first, last = [zero] * n, [zero + 1.0] + [zero] * (n - 1), [zero] * n
    for k in range(1, n):
        low = link[k - 1]
        inv = 1.0 / (main[k] - low * last[k - 1] if k > 1 else main[k])
        base[k] = (source[k] + low * base[k - 1]) * inv if k > 1 else source[k] * inv
        first[k] = low * first[k - 1] * inv
        last[k] = link[k] * inv
    for k in range(n - 2, 0, -1):
        ratio = last[k]
        base[k] = base[k] + ratio * base[k + 1]
        first[k] = first[k] + ratio * first[k + 1]
        last[k] = ratio * last[k + 1]
    return base, first, last


def ends(main, link, source, parts):
    base, first, last = parts
    return [
        main[0] - link[0] * first[1],
        link[0] * last[1],
        source[0] + link[0] * base[1],
        link[-1] - link[-1] * last[-1],
        link[-1] * base[-1],
    ]


def sides(core, field, below, beside):
    row, col = iota(0), iota(1)
    after = jnp.where(row == 7, 0.0, down(field, -1))
    before = jnp.where(row == 0, below, down(field))
    upper = jnp.where(col == 127, jnp.where(core == 0, beside, 0.0), right(field, -1))
    lower = jnp.where(col == 0, jnp.where(core == 0, 0.0, beside), right(field))
    return after, before, upper, lower


def block_kernel(dirn, resid, cond_x, cond_y, cond_z, helmholtz, y_got, diagonal_got, up,
                 spread, own_parts, ext_parts, far_parts, image, lows):
    core = lax.axis_index("gy")
    row, col = iota(0), iota(1)
    n = dirn.shape[0]
    levels = range(n)
    first_row = lambda a: jnp.where(row == 0, a, 0.0)

    own_m, ext_m, far_m, ext_c, ext_r, far_c, far_r = [], [], [], [], [], [], []
    low_xs, low_ys, sides_d, ext_ds = [], [], [], []
    for k in levels:
        cx, cy = cond_x[k], cond_y[k]
        low_x = jnp.where(row == 0, from_below(up, k, 1), down(cx))
        edge = jnp.where(core == 1, far(y_got, k, 1), 0.0)
        low_y = jnp.where(col == 0, edge, right(cy))
        diag = partial_diagonal(k, edge, cond_x, cond_y, cond_z, helmholtz)
        low_xs.append(low_x)
        low_ys.append(low_y)
        own_m.append(diag + first_row(low_x))
        corner = jnp.where(jnp.logical_and(core == 1, col == 0), down(far(diagonal_got, k, 1), 1), 0.0)
        found = first_row(from_below(up, k, 2) + corner)
        ext_m.append(jnp.where(found > 0.0, found, 1.0))
        ext_c.append(first_row(from_below(up, k, 3)))
        ext_r.append(first_row(from_below(up, k, 4)))
        far_m.append(far(y_got, k, 2) + first_row(down(far(diagonal_got, k, 5), 1))
                     + jnp.where(core == 0, lane(cy, 127), 0.0))
        far_c.append(far(y_got, k, 3))
        far_r.append(far(y_got, k, 4))
        ext_ds.append(first_row(from_below(up, k, 0)))
        after, before, upper, lower = sides(core, dirn[k], ext_ds[k], far(y_got, k, 0))
        sides_d.append(cx * after + low_x * before + cy * upper + low_y * lower)
        lows[0, k] = low_x
        lows[1, k] = low_y

    own_c = [cond_z[k] for k in levels]
    own_r = [resid[k] for k in levels]
    own = condense(own_m, own_c, own_r)
    ext = condense(ext_m, ext_c, ext_r)
    beside = condense(far_m, far_c, far_r)
    for ref, parts in ((own_parts, own), (ext_parts, ext), (far_parts, beside)):
        for v in range(3):
            for k in levels:
                ref[v, k] = parts[v][k]

    zero = jnp.zeros((8, 128), jnp.float32)
    c0 = g0 = g1 = g2 = h0 = h1 = h2 = d_ad = r_d = zero
    below_g1 = below_g2 = below_h1 = below_h2 = zero
    quad_x, quad_y = [zero] * 4, [zero] * 4
    flux = zero
    for k in levels:
        d, cx, cy = dirn[k], cond_x[k], cond_y[k]
        low_x, low_y, side = low_xs[k], low_ys[k], sides_d[k]
        b, f, l = own[0][k], own[1][k], own[2][k]
        eb, ef, el = ext[0][k], ext[1][k], ext[2][k]
        face_d, face_b = first_row(low_x * d), first_row(low_x * b)
        below_g1 = below_g1 + face_d * ef
        below_g2 = below_g2 + face_d * el
        g0 = g0 + face_d * eb
        if k:
            after, before, upper, lower = sides(core, b, eb, beside[0][k])
            side_b = cx * after + low_x * before + cy * upper + low_y * lower
            c0 = c0 + resid[k] * b
            g0 = g0 + side * b
            h0 = h0 + side_b * b + face_b * eb
            h1 = h1 + side_b * f
            h2 = h2 + side_b * l
            g2 = g2 + side * l
            below_h1 = below_h1 + face_b * ef
            below_h2 = below_h2 + face_b * el
        g1 = g1 + side * f
        fx = jnp.where(row == 0, ef, down(f))
        lx = jnp.where(row == 0, el, down(l))
        fy = jnp.where(col == 0, beside[1][k], right(f))
        ly = jnp.where(col == 0, beside[2][k], right(l))
        for quad, cond, f_to, l_to in ((quad_x, low_x, fx, lx), (quad_y, low_y, fy, ly)):
            cf, cl = cond * f, cond * l
            for at, term in enumerate((cf * f_to, cf * l_to, cl * f_to, cl * l_to)):
                quad[at] = quad[at] + term
        local = (helmholtz[k] + cx + low_x + cy + low_y) * d - side
        d_ad = d_ad + d * local - face_d * ext_ds[k]
        r_d = r_d + resid[k] * d
        local = local - flux
        if k + 1 < n:
            gap = d - dirn[k + 1]
            flux = cond_z[k] * gap
            d_ad = d_ad + flux * gap
            local = local + flux
        image[k] = local

    chain = ends(own_m, own_c, own_r, own)
    chain_ext = ends(ext_m, ext_c, ext_r, ext)
    chain_far = ends(far_m, far_c, far_r, beside)
    chain_x = [jnp.where(row == 0, e, down(o)) for o, e in zip(chain, chain_ext)]
    chain_y = [jnp.where(col == 0, e, right(o)) for o, e in zip(chain, chain_far)]
    spot = lax.rem(col, WIDTH)
    left = sums = zero
    for v in range(5):
        left = jnp.where(spot == v, right(chain_y[v], v), left)
    for v, part in enumerate((c0, g0, h0, d_ad, r_d)):
        sums = jnp.where(col == v, jnp.sum(part, axis=1, keepdims=True), sums)
    others = ([2.0 * q for q in quad_x] + [2.0 * q for q in quad_y]
              + [2.0 * h1, 2.0 * h2, g1, g2, 2.0 * below_h1, 2.0 * below_h2, below_g1, below_g2]
              + [dirn[0], dirn[n - 1], cond_z[n - 1], left, sums, zero])
    table = [[chain[v], chain_x[v], others[2 * v], others[2 * v + 1]] for v in range(5)]
    table += [others[at:at + 4] for at in (10, 14, 18)]
    block = lax.div(col, WIDTH)
    for quarter in range(QUARTERS):
        for at, values in enumerate(table):
            tile = zero
            for b, value in enumerate(values):
                tile = jnp.where(block == b, right(value, WIDTH * (b - quarter)), tile)
            spread[pl.ds(quarter * ROWS + at, 8, stride=QUARTERS * ROWS), :] = tile


def row_kernel(back, own_parts, dirn, low):
    row = iota(0)
    tiles = [jnp.zeros((8, 128), jnp.float32) for t in range(low.shape[0])]
    for k in range(dirn.shape[0]):
        for v, value in enumerate((own_parts[0, k], own_parts[1, k], own_parts[2, k], dirn[k])):
            at = k * 4 + v
            tiles[at // 8] = jnp.where(row == at % 8, down(value, at % 8), tiles[at // 8])
    for t, tile in enumerate(tiles):
        low[t] = tile


def solver_kernel(rows, back, mains, links, sources, found):
    n = rows.shape[0] // ROWS
    half = n // 2
    lanes = lax.broadcasted_iota(jnp.int32, (n, 128), 1)
    level = lax.broadcasted_iota(jnp.int32, (n, 128), 0)
    take = lambda at: rows[pl.ds(at, n, stride=ROWS), :]
    shift_to = lambda value, by: pltpu.roll(value, by % 128, 1)
    previous = lambda value: jnp.where(level == 0, 0.0, pltpu.roll(value, 1, 0))
    lines = [take(at) for at in range(ROWS)]

    def other(v):
        at, b = (v // 2, 2 + v % 2) if v < 10 else (5 + (v - 10) // 4, (v - 10) % 4)
        return shift_to(lines[at], -b * WIDTH)

    left = other(19)
    chain = []
    for v in range(5):
        value = jnp.where(lanes == LEFT, shift_to(left, LEFT - v), lines[v])
        chain.append(jnp.where(lanes > LEFT, 1.0 if v == 0 else 0.0, value))
    source = chain[2] + previous(chain[4])
    mains[...] = chain[0] + previous(chain[3])
    links[...] = chain[1]
    sources[...] = source
    main = [mains[j:j + 1, :] for j in range(n)]
    link = [links[j:j + 1, :] for j in range(n)]
    src = [sources[j:j + 1, :] for j in range(n)]
    ratio, shift = [None] * n, [None] * n
    for j in range(half):
        a, b = j, n - 1 - j
        if j:
            inv_a = 1.0 / (main[a] - link[a - 1] * ratio[a - 1])
            inv_b = 1.0 / (main[b] - link[b] * ratio[b + 1])
            shift[a] = (src[a] + link[a - 1] * shift[a - 1]) * inv_a
            shift[b] = (src[b] + link[b] * shift[b + 1]) * inv_b
        else:
            inv_a, inv_b = 1.0 / main[a], 1.0 / main[b]
            shift[a], shift[b] = src[a] * inv_a, src[b] * inv_b
        ratio[a] = link[a] * inv_a
        ratio[b] = link[b - 1] * inv_b
    x = [None] * n
    a, b = half - 1, half
    x[a] = (shift[a] + ratio[a] * shift[b]) / (1.0 - ratio[a] * ratio[b])
    x[b] = shift[b] + ratio[b] * x[a]
    for j in range(half - 2, -1, -1):
        x[j] = shift[j] + ratio[j] * x[j + 1]
        m = n - 1 - j
        x[m] = shift[m] + ratio[m] * x[m - 1]
    for j in range(n):
        found[j:j + 1, :] = x[j]

    x = found[...]
    x2 = jnp.where(level == n - 1, 0.0, pltpu.roll(x, n - 1, 0))
    below, below2 = shift_to(x, -WIDTH), shift_to(x2, -WIDTH)
    beside = jnp.where(lanes == 0, shift_to(x, -LEFT), shift_to(x, 1))
    beside2 = jnp.where(lanes == 0, shift_to(x2, -LEFT), shift_to(x2, 1))
    quad = (x * (other(0) * below + other(1) * below2 + other(4) * beside + other(5) * beside2)
            + x2 * (other(2) * below + other(3) * below2 + other(6) * beside + other(7) * beside2))
    sum_h = quad + x * other(8) + x2 * other(9) + below * other(12) + below2 * other(13)
    sum_g = x * other(10) + x2 * other(11) + below * other(14) + below2 * other(15)
    gap = other(17) - jnp.where(level == n - 1, 0.0, pltpu.roll(other(16), n - 1, 0))
    flux = other(18) * gap
    amounts = [x * source, sum_g, sum_h, flux * gap, None]
    known = jnp.sum(other(20), axis=0, keepdims=True)
    lane_row = lax.broadcasted_iota(jnp.int32, (1, 128), 1)
    scalars = jnp.where(lane_row < 5, known, 0.0)
    for v, amount in enumerate(amounts[:4]):
        amount = jnp.where(lane_row < WIDTH, jnp.sum(amount, axis=0, keepdims=True), 0.0)
        scalars = scalars + jnp.where(lane_row == v, jnp.sum(amount, axis=1, keepdims=True), 0.0)
    scalars = jnp.broadcast_to(pltpu.roll(jnp.broadcast_to(scalars, (8, 128)), SUMS, 1)[0:1, :], (n, 128))
    in_flux = jnp.logical_and(lanes >= FLUX, lanes < SUMS)
    tail = jnp.where(lanes >= SUMS, scalars, 0.0)
    back[pl.ds(0, n, stride=BACK), :] = jnp.where(
        lanes <= LEFT, x, jnp.where(in_flux, shift_to(previous(flux), FLUX), tail))
    back[pl.ds(1, n, stride=BACK), :] = jnp.where(lanes <= LEFT, x2, jnp.where(in_flux, shift_to(flux, FLUX), tail))


def scalar_kernel(tops, got, spread):
    n = got.shape[0] // BACK
    amount = jnp.sum(got[pl.ds(0, n, stride=BACK), :], axis=0, keepdims=True)
    for t in range(spread.shape[0]):
        spread[t, 0:1, :] = amount
        spread[t, 1:3, :] = tops[0:2, :]
        spread[t, 3:4, :] = amount


def column_kernel(low, got, resid, cond_x, cond_y, own_parts, ext_parts, far_parts, image_in, lows,
                  precond, image_p, image_d, tops):
    core = lax.axis_index("gy")
    n = resid.shape[0]
    block = lax.div(iota(1), WIDTH)
    part = lambda quarter, v: got[pl.ds(quarter * BACK + v, 8, stride=QUARTERS * BACK), :]

    def gather(v, lane_from):
        tile = jnp.zeros((8, 128), jnp.float32)
        for quarter in range(QUARTERS):
            tile = jnp.where(block == quarter, right(part(quarter, v), WIDTH * quarter - lane_from), tile)
        return tile

    x, x2 = gather(0, 0), gather(1, 0)
    ext_x, ext_x2 = gather(0, WIDTH), gather(1, WIDTH)
    far_x, far_x2 = lane(part(0, 0), LEFT), lane(part(0, 1), LEFT)
    flux_below, flux_above = gather(0, FLUX), gather(1, FLUX)
    tops[...] = jnp.where(iota(0) == 0, x, down(x2))
    join = lambda parts, k, a, b: parts[0, k] + a * parts[1, k] + b * parts[2, k]
    for k in range(n):
        p = join(own_parts, k, x, x2)
        ext = join(ext_parts, k, ext_x, ext_x2)
        beside = join(far_parts, k, far_x, far_x2)
        after, before, upper, lower = sides(core, p, ext, beside)
        side = cond_x[k] * after + lows[0, k] * before + cond_y[k] * upper + lows[1, k] * lower
        precond[k] = p
        image_p[k] = resid[k] - side
        local = image_in[k]
        if k == 0:
            local = local - flux_below
        if k == n - 1:
            local = local + flux_above
        image_d[k] = local


def update_kernel(scalars, low, cond_x, sol, resid, dirn, precond, image_p, image_d,
                  sol_out, res_out, dir_out):
    row = iota(0)
    amount = jnp.sum(scalars[:, 0, :], axis=0, keepdims=True)
    per_row = lax.axis_size("gy")
    mate = lax.axis_index("gx") * per_row + lax.axis_index("gy") + per_row
    mate = jnp.minimum(mate, scalars.shape[0] - 1)
    x, x2 = (jnp.broadcast_to(scalars[mate, v:v + 1, :], (8, 128)) for v in (1, 2))
    r_p, p_nd, p_np, d_ad, r_d = (jnp.broadcast_to(amount[:, v:v + 1], (8, 128)) for v in range(SUMS, SUMS + 5))
    p_ad = r_d - p_nd
    conj = -p_ad / d_ad
    step = (r_p + conj * r_d) / (r_p - p_np + conj * p_ad)
    for k in range(sol.shape[0]):
        out = precond[k] + conj * dirn[k]
        dir_out[k] = out
        sol_out[k] = sol[k] + step * out
        b_up, f_up, l_up, d_up = (down(low[(4 * k + v) // 8], 7 - (4 * k + v) % 8) for v in range(4))
        p_up = b_up + x * f_up + x2 * l_up
        above = jnp.where(row == 7, cond_x[k] * (p_up + conj * d_up), 0.0)
        res_out[k] = resid[k] - step * (image_p[k] + conj * image_d[k] - above)


def call(kernel, outs, *args, scratch=(), first=0):
    many = isinstance(outs, tuple)
    return pl.pallas_call(
        kernel, out_shape=outs, in_specs=[ANY] * first + [VMEM] * (len(args) - first),
        out_specs=(VMEM,) * len(outs) if many else VMEM, scratch_shapes=scratch,
        compiler_params=pltpu.CompilerParams(vmem_limit_bytes=8 << 20))(*args)


def body(solution_in, residual_in, direction_in, cond_x, cond_y, cond_z, helmholtz):
    nz, nx, ny = direction_in.shape
    gz, gx = lax.axis_size("gz"), lax.axis_size("gx")
    mates = gx * lax.axis_size("gy")
    field = shape(nz, nx, ny)
    parts = shape(3, nz, nx, ny)
    given = [pltpu.with_memory_space_constraint(a, pltpu.HBM)
             for a in (direction_in, residual_in, cond_x, cond_y, cond_z, helmholtz)]

    y_face, x_face, *given = call(
        face_kernel, (shape(-(-nz // 16), nx, ny), shape(nz * 5 // 8, nx, ny)) + (field,) * 6, *given,
        scratch=(pltpu.SemaphoreType.DMA((6 * PARTS,)),), first=6)
    direction_in, residual_in, cond_x, cond_y, cond_z, helmholtz = given
    up = shifted(x_face, "gx", 1)
    y_got = lax.ppermute(y_face, "gy", [(0, 1), (1, 0)])
    diagonal_got = lax.ppermute(y_face, ("gx", "gy"), [
        (2 * i + c, 2 * i + 3 - c) for i in range(gx - 1) for c in range(2)])
    spread, own_parts, ext_parts, far_parts, image, lows = call(
        block_kernel, (shape(gz * ROWS, ny), parts, parts, parts, field, shape(2, nz, nx, ny)),
        *given, y_got, diagonal_got, up)
    rows = lax.all_to_all(spread.reshape(gz, ROWS, ny), "gz", 0, 0, tiled=True)
    back = call(solver_kernel, shape(gz * BACK, ny), rows.reshape(gz * ROWS, ny),
                scratch=(pltpu.VMEM((gz, ny), jnp.float32),) * 4)
    low = call(row_kernel, shape(nz // 2, nx, ny), back, own_parts, direction_in, first=1)
    low = shifted(low, "gx", -1)
    got = lax.all_to_all(back.reshape(gz, BACK, ny), "gz", 0, 0, tiled=True).reshape(gz * BACK, ny)
    precond, image_p, image_d, tops = call(
        column_kernel, (field, field, field, shape(8, ny)), low, got, residual_in, cond_x, cond_y,
        own_parts, ext_parts, far_parts, image, lows, first=1)
    sums = call(scalar_kernel, shape(mates, 4, ny), tops, got)
    sums = lax.all_to_all(sums, ("gx", "gy"), 0, 0, tiled=True)
    return call(update_kernel, (field, field, field), sums, low, cond_x, solution_in, residual_in, direction_in,
                precond, image_p, image_d)


def solution(mesh):
    spec = P("gz", "gx", "gy")
    return jax.shard_map(body, mesh=mesh, in_specs=(spec,) * 7, out_specs=(spec,) * 3, check_vma=False)
```

```python
import jax
import jax.numpy as jnp
from jax import lax
from jax.experimental import pallas as pl
from jax.experimental.pallas import tpu as pltpu
from jax.sharding import PartitionSpec as P

PARTS = 2
QUARTERS = 4
WIDTH = 128 // QUARTERS
ROWS = 8
BACK = 2
LEFT = 2 * WIDTH
FLUX = LEFT + 1
SUMS = FLUX + WIDTH
VMEM = pl.BlockSpec(memory_space=pltpu.VMEM)
ANY = pl.BlockSpec(memory_space=pl.ANY)


def shape(*dims):
    return jax.ShapeDtypeStruct(dims, jnp.float32)


def shifted(value, axis, by):
    count = lax.axis_size(axis)
    return lax.ppermute(value, axis, [(i, i + by) for i in range(count) if 0 <= i + by < count])


def iota(axis):
    return lax.broadcasted_iota(jnp.int32, (8, 128), axis)


def down(tile, by=1):
    return pltpu.roll(tile, by % 8, 0)


def right(tile, by=1):
    return pltpu.roll(tile, by % 128, 1)


def lane(tile, at):
    return jnp.broadcast_to(tile[:, at:at + 1], (8, 128))


def far(y_got, k, v):
    return lane(y_got[k // 16], k % 16 * 8 + v)


def from_below(up, k, v, to=0):
    at = k * 5 + v
    return down(up[at // 8], to - at % 8)


def partial_diagonal(k, edge, cond_x, cond_y, cond_z, helmholtz):
    row, col = iota(0), iota(1)
    cx, cy = cond_x[k], cond_y[k]
    low_y = jnp.where(col == 0, edge, right(cy))
    low_x = jnp.where(row == 0, 0.0, down(cx))
    total = helmholtz[k] + cx + low_x + cy + low_y + cond_z[k]
    return total + cond_z[k - 1] if k else total


def face_kernel(*refs):
    given, y_face, x_face, held, sems = refs[:6], refs[6], refs[7], refs[8:14], refs[14]
    n = given[0].shape[0]
    size = 2 * n // 3
    copies = []
    for part in range(PARTS):
        levels = pl.ds(0, size) if part == 0 else pl.ds(size, n - size)
        for a, (src, dst) in enumerate(zip(given, held)):
            copies.append(pltpu.make_async_copy(src.at[levels], dst.at[levels], sems.at[6 * part + a]))
            copies[-1].start()
    dirn, resid, cond_x, cond_y, cond_z, helmholtz = held
    row, col = iota(0), iota(1)
    face = 127 - 127 * lax.axis_index("gy")
    y_tiles = [jnp.zeros((8, 128), jnp.float32) for t in range(y_face.shape[0])]
    x_tiles = [jnp.zeros((8, 128), jnp.float32) for t in range(x_face.shape[0])]
    for k in range(n):
        if k % size == 0:
            for copy in copies[6 * (k // size):6 * (k // size) + 6]:
                copy.wait()
        diag = partial_diagonal(k, 0.0, cond_x, cond_y, cond_z, helmholtz)
        for v, value in enumerate((dirn[k], cond_y[k], diag, cond_z[k], resid[k], cond_x[k])):
            at = k % 16 * 8 + v
            moved = pltpu.roll(value, lax.rem(at - face + 256, 128), 1)
            y_tiles[k // 16] = jnp.where(col == at, moved, y_tiles[k // 16])
        for v, value in enumerate((dirn[k], cond_x[k], diag, cond_z[k], resid[k])):
            at = k * 5 + v
            x_tiles[at // 8] = jnp.where(row == at % 8, down(value, at % 8 - 7), x_tiles[at // 8])
    for ref, tiles in ((y_face, y_tiles), (x_face, x_tiles)):
        for t, tile in enumerate(tiles):
            ref[t] = tile


def condense(main, link, source):
    n = len(main)
    zero = jnp.zeros_like(main[0])
    base, first, last = [zero] * n, [zero + 1.0] + [zero] * (n - 1), [zero] * n
    for k in range(1, n):
        low = link[k - 1]
        inv = 1.0 / (main[k] - low * last[k - 1] if k > 1 else main[k])
        base[k] = (source[k] + low * base[k - 1]) * inv if k > 1 else source[k] * inv
        first[k] = low * first[k - 1] * inv
        last[k] = link[k] * inv
    for k in range(n - 2, 0, -1):
        ratio = last[k]
        base[k] = base[k] + ratio * base[k + 1]
        first[k] = first[k] + ratio * first[k + 1]
        last[k] = ratio * last[k + 1]
    return base, first, last


def ends(main, link, source, parts):
    base, first, last = parts
    return [
        main[0] - link[0] * first[1],
        link[0] * last[1],
        source[0] + link[0] * base[1],
        link[-1] - link[-1] * last[-1],
        link[-1] * base[-1],
    ]


def sides(core, field, below, beside):
    row, col = iota(0), iota(1)
    after = jnp.where(row == 7, 0.0, down(field, -1))
    before = jnp.where(row == 0, below, down(field))
    upper = jnp.where(col == 127, jnp.where(core == 0, beside, 0.0), right(field, -1))
    lower = jnp.where(col == 0, jnp.where(core == 0, 0.0, beside), right(field))
    return after, before, upper, lower


def block_kernel(dirn, resid, cond_x, cond_y, cond_z, helmholtz, y_got, diagonal_got, up,
                 spread, own_parts, ext_parts, far_parts, image, lows):
    core = lax.axis_index("gy")
    row, col = iota(0), iota(1)
    n = dirn.shape[0]
    levels = range(n)
    first_row = lambda a: jnp.where(row == 0, a, 0.0)

    own_m, ext_m, far_m, ext_c, ext_r, far_c, far_r = [], [], [], [], [], [], []
    low_xs, low_ys, sides_d, ext_ds = [], [], [], []
    for k in levels:
        cx, cy = cond_x[k], cond_y[k]
        low_x = jnp.where(row == 0, from_below(up, k, 1), down(cx))
        edge = jnp.where(core == 1, far(y_got, k, 1), 0.0)
        low_y = jnp.where(col == 0, edge, right(cy))
        diag = partial_diagonal(k, edge, cond_x, cond_y, cond_z, helmholtz)
        low_xs.append(low_x)
        low_ys.append(low_y)
        own_m.append(diag + first_row(low_x))
        corner = jnp.where(jnp.logical_and(core == 1, col == 0), down(far(diagonal_got, k, 1), 1), 0.0)
        found = first_row(from_below(up, k, 2) + corner)
        ext_m.append(jnp.where(found > 0.0, found, 1.0))
        ext_c.append(first_row(from_below(up, k, 3)))
        ext_r.append(first_row(from_below(up, k, 4)))
        far_m.append(far(y_got, k, 2) + first_row(down(far(diagonal_got, k, 5), 1))
                     + jnp.where(core == 0, lane(cy, 127), 0.0))
        far_c.append(far(y_got, k, 3))
        far_r.append(far(y_got, k, 4))
        ext_ds.append(first_row(from_below(up, k, 0)))
        after, before, upper, lower = sides(core, dirn[k], ext_ds[k], far(y_got, k, 0))
        sides_d.append(cx * after + low_x * before + cy * upper + low_y * lower)
        lows[0, k] = low_x
        lows[1, k] = low_y

    own_c = [cond_z[k] for k in levels]
    own_r = [resid[k] for k in levels]
    own = condense(own_m, own_c, own_r)
    ext = condense(ext_m, ext_c, ext_r)
    beside = condense(far_m, far_c, far_r)
    for ref, parts in ((own_parts, own), (ext_parts, ext), (far_parts, beside)):
        for v in range(3):
            for k in levels:
                ref[v, k] = parts[v][k]

    zero = jnp.zeros((8, 128), jnp.float32)
    c0 = g0 = g1 = g2 = h0 = h1 = h2 = d_ad = r_d = zero
    below_g1 = below_g2 = below_h1 = below_h2 = zero
    quad_x, quad_y = [zero] * 4, [zero] * 4
    flux = zero
    for k in levels:
        d, cx, cy = dirn[k], cond_x[k], cond_y[k]
        low_x, low_y, side = low_xs[k], low_ys[k], sides_d[k]
        b, f, l = own[0][k], own[1][k], own[2][k]
        eb, ef, el = ext[0][k], ext[1][k], ext[2][k]
        face_d, face_b = first_row(low_x * d), first_row(low_x * b)
        below_g1 = below_g1 + face_d * ef
        below_g2 = below_g2 + face_d * el
        g0 = g0 + face_d * eb
        if k:
            after, before, upper, lower = sides(core, b, eb, beside[0][k])
            side_b = cx * after + low_x * before + cy * upper + low_y * lower
            c0 = c0 + resid[k] * b
            g0 = g0 + side * b
            h0 = h0 + side_b * b + face_b * eb
            h1 = h1 + side_b * f
            h2 = h2 + side_b * l
            g2 = g2 + side * l
            below_h1 = below_h1 + face_b * ef
            below_h2 = below_h2 + face_b * el
        g1 = g1 + side * f
        fx = jnp.where(row == 0, ef, down(f))
        lx = jnp.where(row == 0, el, down(l))
        fy = jnp.where(col == 0, beside[1][k], right(f))
        ly = jnp.where(col == 0, beside[2][k], right(l))
        for quad, cond, f_to, l_to in ((quad_x, low_x, fx, lx), (quad_y, low_y, fy, ly)):
            cf, cl = cond * f, cond * l
            for at, term in enumerate((cf * f_to, cf * l_to, cl * f_to, cl * l_to)):
                quad[at] = quad[at] + term
        local = (helmholtz[k] + cx + low_x + cy + low_y) * d - side
        d_ad = d_ad + d * local - face_d * ext_ds[k]
        r_d = r_d + resid[k] * d
        local = local - flux
        if k + 1 < n:
            gap = d - dirn[k + 1]
            flux = cond_z[k] * gap
            d_ad = d_ad + flux * gap
            local = local + flux
        image[k] = local

    chain = ends(own_m, own_c, own_r, own)
    chain_ext = ends(ext_m, ext_c, ext_r, ext)
    chain_far = ends(far_m, far_c, far_r, beside)
    chain_x = [jnp.where(row == 0, e, down(o)) for o, e in zip(chain, chain_ext)]
    chain_y = [jnp.where(col == 0, e, right(o)) for o, e in zip(chain, chain_far)]
    spot = lax.rem(col, WIDTH)
    left = sums = zero
    for v in range(5):
        left = jnp.where(spot == v, right(chain_y[v], v), left)
    for v, part in enumerate((c0, g0, h0, d_ad, r_d)):
        sums = jnp.where(col == v, jnp.sum(part, axis=1, keepdims=True), sums)
    others = ([2.0 * q for q in quad_x] + [2.0 * q for q in quad_y]
              + [2.0 * h1, 2.0 * h2, g1, g2, 2.0 * below_h1, 2.0 * below_h2, below_g1, below_g2]
              + [dirn[0], dirn[n - 1], cond_z[n - 1], left, sums, zero])
    table = [[chain[v], chain_x[v], others[2 * v], others[2 * v + 1]] for v in range(5)]
    table += [others[at:at + 4] for at in (10, 14, 18)]
    block = lax.div(col, WIDTH)
    for quarter in range(QUARTERS):
        for at, values in enumerate(table):
            tile = zero
            for b, value in enumerate(values):
                tile = jnp.where(block == b, right(value, WIDTH * (b - quarter)), tile)
            spread[pl.ds(quarter * ROWS + at, 8, stride=QUARTERS * ROWS), :] = tile


def row_kernel(back, own_parts, dirn, low):
    row = iota(0)
    tiles = [jnp.zeros((8, 128), jnp.float32) for t in range(low.shape[0])]
    for k in range(dirn.shape[0]):
        for v, value in enumerate((own_parts[0, k], own_parts[1, k], own_parts[2, k], dirn[k])):
            at = k * 4 + v
            tiles[at // 8] = jnp.where(row == at % 8, down(value, at % 8), tiles[at // 8])
    for t, tile in enumerate(tiles):
        low[t] = tile


def solver_kernel(rows, back, mains, links, sources, found):
    n = rows.shape[0] // ROWS
    half = n // 2
    lanes = lax.broadcasted_iota(jnp.int32, (n, 128), 1)
    level = lax.broadcasted_iota(jnp.int32, (n, 128), 0)
    take = lambda at: rows[pl.ds(at, n, stride=ROWS), :]
    shift_to = lambda value, by: pltpu.roll(value, by % 128, 1)
    previous = lambda value: jnp.where(level == 0, 0.0, pltpu.roll(value, 1, 0))
    lines = [take(at) for at in range(ROWS)]

    def other(v):
        at, b = (v // 2, 2 + v % 2) if v < 10 else (5 + (v - 10) // 4, (v - 10) % 4)
        return shift_to(lines[at], -b * WIDTH)

    left = other(19)
    chain = []
    for v in range(5):
        value = jnp.where(lanes == LEFT, shift_to(left, LEFT - v), lines[v])
        chain.append(jnp.where(lanes > LEFT, 1.0 if v == 0 else 0.0, value))
    source = chain[2] + previous(chain[4])
    mains[...] = chain[0] + previous(chain[3])
    links[...] = chain[1]
    sources[...] = source
    main = [mains[j:j + 1, :] for j in range(n)]
    link = [links[j:j + 1, :] for j in range(n)]
    src = [sources[j:j + 1, :] for j in range(n)]
    ratio, shift = [None] * n, [None] * n
    for j in range(half):
        a, b = j, n - 1 - j
        if j:
            inv_a = 1.0 / (main[a] - link[a - 1] * ratio[a - 1])
            inv_b = 1.0 / (main[b] - link[b] * ratio[b + 1])
            shift[a] = (src[a] + link[a - 1] * shift[a - 1]) * inv_a
            shift[b] = (src[b] + link[b] * shift[b + 1]) * inv_b
        else:
            inv_a, inv_b = 1.0 / main[a], 1.0 / main[b]
            shift[a], shift[b] = src[a] * inv_a, src[b] * inv_b
        ratio[a] = link[a] * inv_a
        ratio[b] = link[b - 1] * inv_b
    x = [None] * n
    a, b = half - 1, half
    x[a] = (shift[a] + ratio[a] * shift[b]) / (1.0 - ratio[a] * ratio[b])
    x[b] = shift[b] + ratio[b] * x[a]
    for j in range(half - 2, -1, -1):
        x[j] = shift[j] + ratio[j] * x[j + 1]
        m = n - 1 - j
        x[m] = shift[m] + ratio[m] * x[m - 1]
    for j in range(n):
        found[j:j + 1, :] = x[j]

    x = found[...]
    x2 = jnp.where(level == n - 1, 0.0, pltpu.roll(x, n - 1, 0))
    below, below2 = shift_to(x, -WIDTH), shift_to(x2, -WIDTH)
    beside = jnp.where(lanes == 0, shift_to(x, -LEFT), shift_to(x, 1))
    beside2 = jnp.where(lanes == 0, shift_to(x2, -LEFT), shift_to(x2, 1))
    quad = (x * (other(0) * below + other(1) * below2 + other(4) * beside + other(5) * beside2)
            + x2 * (other(2) * below + other(3) * below2 + other(6) * beside + other(7) * beside2))
    sum_h = quad + x * other(8) + x2 * other(9) + below * other(12) + below2 * other(13)
    sum_g = x * other(10) + x2 * other(11) + below * other(14) + below2 * other(15)
    gap = other(17) - jnp.where(level == n - 1, 0.0, pltpu.roll(other(16), n - 1, 0))
    flux = other(18) * gap
    amounts = [x * source, sum_g, sum_h, flux * gap, None]
    known = jnp.sum(other(20), axis=0, keepdims=True)
    lane_row = lax.broadcasted_iota(jnp.int32, (1, 128), 1)
    scalars = jnp.where(lane_row < 5, known, 0.0)
    for v, amount in enumerate(amounts[:4]):
        amount = jnp.where(lane_row < WIDTH, jnp.sum(amount, axis=0, keepdims=True), 0.0)
        scalars = scalars + jnp.where(lane_row == v, jnp.sum(amount, axis=1, keepdims=True), 0.0)
    scalars = jnp.broadcast_to(pltpu.roll(jnp.broadcast_to(scalars, (8, 128)), SUMS, 1)[0:1, :], (n, 128))
    in_flux = jnp.logical_and(lanes >= FLUX, lanes < SUMS)
    tail = jnp.where(lanes >= SUMS, scalars, 0.0)
    back[pl.ds(0, n, stride=BACK), :] = jnp.where(
        lanes <= LEFT, x, jnp.where(in_flux, shift_to(previous(flux), FLUX), tail))
    back[pl.ds(1, n, stride=BACK), :] = jnp.where(lanes <= LEFT, x2, jnp.where(in_flux, shift_to(flux, FLUX), tail))


def scalar_kernel(tops, got, spread):
    n = got.shape[0] // BACK
    amount = jnp.sum(got[pl.ds(0, n, stride=BACK), :], axis=0, keepdims=True)
    for t in range(spread.shape[0]):
        spread[t, 0:1, :] = amount
        spread[t, 1:3, :] = tops[0:2, :]
        spread[t, 3:4, :] = amount


def column_kernel(low, got, resid, cond_x, cond_y, own_parts, ext_parts, far_parts, image_in, lows,
                  precond, image_p, image_d, tops):
    core = lax.axis_index("gy")
    n = resid.shape[0]
    block = lax.div(iota(1), WIDTH)
    part = lambda quarter, v: got[pl.ds(quarter * BACK + v, 8, stride=QUARTERS * BACK), :]

    def gather(v, lane_from):
        tile = jnp.zeros((8, 128), jnp.float32)
        for quarter in range(QUARTERS):
            tile = jnp.where(block == quarter, right(part(quarter, v), WIDTH * quarter - lane_from), tile)
        return tile

    x, x2 = gather(0, 0), gather(1, 0)
    ext_x, ext_x2 = gather(0, WIDTH), gather(1, WIDTH)
    far_x, far_x2 = lane(part(0, 0), LEFT), lane(part(0, 1), LEFT)
    flux_below, flux_above = gather(0, FLUX), gather(1, FLUX)
    tops[...] = jnp.where(iota(0) == 0, x, down(x2))
    join = lambda parts, k, a, b: parts[0, k] + a * parts[1, k] + b * parts[2, k]
    for k in range(n):
        p = join(own_parts, k, x, x2)
        ext = join(ext_parts, k, ext_x, ext_x2)
        beside = join(far_parts, k, far_x, far_x2)
        after, before, upper, lower = sides(core, p, ext, beside)
        side = cond_x[k] * after + lows[0, k] * before + cond_y[k] * upper + lows[1, k] * lower
        precond[k] = p
        image_p[k] = resid[k] - side
        local = image_in[k]
        if k == 0:
            local = local - flux_below
        if k == n - 1:
            local = local + flux_above
        image_d[k] = local


def update_kernel(scalars, low, cond_x, sol, resid, dirn, precond, image_p, image_d,
                  sol_out, res_out, dir_out):
    row = iota(0)
    amount = jnp.sum(scalars[:, 0, :], axis=0, keepdims=True)
    per_row = lax.axis_size("gy")
    mate = lax.axis_index("gx") * per_row + lax.axis_index("gy") + per_row
    mate = jnp.minimum(mate, scalars.shape[0] - 1)
    x, x2 = (jnp.broadcast_to(scalars[mate, v:v + 1, :], (8, 128)) for v in (1, 2))
    r_p, p_nd, p_np, d_ad, r_d = (jnp.broadcast_to(amount[:, v:v + 1], (8, 128)) for v in range(SUMS, SUMS + 5))
    p_ad = r_d - p_nd
    conj = -p_ad / d_ad
    step = (r_p + conj * r_d) / (r_p - p_np + conj * p_ad)
    for k in range(sol.shape[0]):
        out = precond[k] + conj * dirn[k]
        dir_out[k] = out
        sol_out[k] = sol[k] + step * out
        b_up, f_up, l_up, d_up = (down(low[(4 * k + v) // 8], 7 - (4 * k + v) % 8) for v in range(4))
        p_up = b_up + x * f_up + x2 * l_up
        above = jnp.where(row == 7, cond_x[k] * (p_up + conj * d_up), 0.0)
        res_out[k] = resid[k] - step * (image_p[k] + conj * image_d[k] - above)


def call(kernel, outs, *args, scratch=(), first=0):
    many = isinstance(outs, tuple)
    return pl.pallas_call(
        kernel, out_shape=outs, in_specs=[ANY] * first + [VMEM] * (len(args) - first),
        out_specs=(VMEM,) * len(outs) if many else VMEM, scratch_shapes=scratch,
        compiler_params=pltpu.CompilerParams(vmem_limit_bytes=8 << 20))(*args)


def body(solution_in, residual_in, direction_in, cond_x, cond_y, cond_z, helmholtz):
    nz, nx, ny = direction_in.shape
    gz, gx = lax.axis_size("gz"), lax.axis_size("gx")
    mates = gx * lax.axis_size("gy")
    field = shape(nz, nx, ny)
    parts = shape(3, nz, nx, ny)
    given = [pltpu.with_memory_space_constraint(a, pltpu.HBM)
             for a in (direction_in, residual_in, cond_x, cond_y, cond_z, helmholtz)]

    y_face, x_face, *given = call(
        face_kernel, (shape(-(-nz // 16), nx, ny), shape(nz * 5 // 8, nx, ny)) + (field,) * 6, *given,
        scratch=(pltpu.SemaphoreType.DMA((6 * PARTS,)),), first=6)
    direction_in, residual_in, cond_x, cond_y, cond_z, helmholtz = given
    up = shifted(x_face, "gx", 1)
    y_got = lax.ppermute(y_face, "gy", [(0, 1), (1, 0)])
    diagonal_got = lax.ppermute(y_face, ("gx", "gy"), [
        (2 * i + c, 2 * i + 3 - c) for i in range(gx - 1) for c in range(2)])
    spread, own_parts, ext_parts, far_parts, image, lows = call(
        block_kernel, (shape(gz * ROWS, ny), parts, parts, parts, field, shape(2, nz, nx, ny)),
        *given, y_got, diagonal_got, up)
    rows = lax.all_to_all(spread.reshape(gz, ROWS, ny), "gz", 0, 0, tiled=True)
    back = call(solver_kernel, shape(gz * BACK, ny), rows.reshape(gz * ROWS, ny),
                scratch=(pltpu.VMEM((gz, ny), jnp.float32),) * 4)
    low = call(row_kernel, shape(nz // 2, nx, ny), back, own_parts, direction_in, first=1)
    low = shifted(low, "gx", -1)
    got = lax.all_to_all(back.reshape(gz, BACK, ny), "gz", 0, 0, tiled=True).reshape(gz * BACK, ny)
    precond, image_p, image_d, tops = call(
        column_kernel, (field, field, field, shape(8, ny)), low, got, residual_in, cond_x, cond_y,
        own_parts, ext_parts, far_parts, image, lows, first=1)
    sums = call(scalar_kernel, shape(mates, 4, ny), tops, got)
    sums = lax.all_to_all(sums, ("gx", "gy"), 0, 0, tiled=True)
    return call(update_kernel, (field, field, field), sums, low, cond_x, solution_in, residual_in, direction_in,
                precond, image_p, image_d)


def solution(mesh):
    spec = P("gz", "gx", "gy")
    return jax.shard_map(body, mesh=mesh, in_specs=(spec,) * 7, out_specs=(spec,) * 3, check_vma=False)
```
